32 devices in a mesh: group: 2 (over x), ep: 16 (over z, y, core).
Axes of the slice: x: 2, y: 2, z: 4, core: 2. Of those that a mesh axis runs over, the one named last changes fastest.
Arguments:
- hidden: bfloat16 [4096, 2048], P(('group', 'ep')), parts along dimension 0, may hold values from -6 to 6
- norm_gain: float32 [2048], replicated, may hold values from 0.25 to 4
- routes: int32 [4096, 8], P(('group', 'ep')), parts along dimension 0, may hold values from 0 to 15, all different within a row; in each aligned block of 128 rows (0 to 127, 128 to 255, ...) at most 80 rows name the same one
- route_weight: float32 [4096, 8], P(('group', 'ep')), parts along dimension 0, may hold values from 0.05 to 1
- w_gate: bfloat16 [16, 2048, 768], P('ep'), may hold values from -0.125 to 0.125
- w_up: bfloat16 [16, 2048, 768], P('ep'), may hold values from -0.125 to 0.125
- w_down: bfloat16 [16, 768, 2048], P('ep'), may hold values from -0.21875 to 0.21875
Outputs:
- mixed: bfloat16 [4096, 2048], P(('group', 'ep')), parts along dimension 0
The draws below stay inside these ranges and needn't reach their ends.
There are 2 independent parts, one for each index of `group`. The reference program is written for one: setup_inputs(seed, part) draws one part's arguments, and reference() takes and returns one part's arrays. A program takes and returns all parts, laid end to end along the dimension named above; an argument that names none is the same for every part. Nothing has to cross between parts.
Inputs may be any that keep to these rules, and one draw needn't show every extreme that they name: `routes`: each row names 8 different experts. Among the rows of one device no expert is named more than 80 times, a bound that some block reaches.
All inputs are finite; a program needn't handle non-finite values.
Results may differ from the reference program's by a relative error of at most 0.0085.
Values may be sent and summed in bfloat16 or wider, within the bound.
No kernel may reach another device: no remote copies, remote signals or barrier semaphores. Data moves between devices by JAX's collectives and lax.ppermute only.
A program may use at most 128 MiB of HBM per device.

```python
import math
import jax
import jax.numpy as jnp
import numpy as np
from jax import lax

D = 2048
FF = 768
TOP = 8
TOK_DEV = 128
EXPERTS = 16
TOKENS = 2048
CAP = 80
N_EP = 16


def block_levels(stream_key, shape, pieces, low, top_value):
    def one(dim, parts):
        draws = jax.random.uniform(jax.random.fold_in(jax.random.fold_in(stream_key, 6), dim), (parts,), jnp.float32, low / len(pieces), top_value / len(pieces))
        return jnp.repeat(jnp.exp(draws), shape[dim] // parts).reshape((-1,) + (1,) * (len(shape) - dim - 1))

    factor_of = one(*pieces[0])
    for cut in pieces[1:]:
        factor_of = factor_of * one(*cut)
    return factor_of


def shared_out(key, own, number, rows, amount, top, limit, lean):
    ranking = jax.random.permutation(key, amount)
    crowded, usual = load_shares(amount, rows * top, limit, lean, True), load_shares(amount, rows * top, limit, lean, False)
    places = jnp.arange(amount)

    def named(sizes, turn):
        used = int((sizes > 0).sum())
        fixed = max(1, used // 4)
        shifted = fixed + (places - fixed + turn * (used - fixed)) % max(1, amount - fixed)
        return jnp.zeros((amount,), jnp.int32).at[ranking[jnp.where(places < fixed, places, shifted)]].set(jnp.asarray(sizes, jnp.int32))

    sizes = jnp.where(number % 4 == 0, named(crowded, number // 4), named(usual, number - number // 4 - 1))
    mixed = jax.random.permutation(jax.random.fold_in(own, 3), amount)
    giver, taker = mixed[0:amount // 2 * 2:2], mixed[1:amount // 2 * 2:2]
    room = jnp.minimum(sizes[giver] - 1, limit - sizes[taker]) // 2
    room = jnp.where((giver == ranking[0]) | (taker == ranking[0]) | (sizes[taker] == 0), 0, jnp.maximum(room, 0))
    shifted = jax.random.randint(jax.random.fold_in(own, 4), (amount // 2,), 0, 1 << 20) % (room + 1)
    sizes = sizes.at[giver].add(-shifted).at[taker].add(shifted)
    labels = jnp.searchsorted(jnp.cumsum(sizes), jnp.arange(rows * top), side="right").astype(jnp.int32)
    grid = labels.reshape(top, rows).T
    grid = grid[jax.random.permutation(jax.random.fold_in(own, 1), rows)]
    turn = jax.random.randint(jax.random.fold_in(own, 2), (rows, 1), 0, top)
    return jnp.take_along_axis(grid, (jnp.arange(top)[None, :] + turn) % top, axis=1)


def load_shares(number_of, total, most, slope, full):
    loads = [(1 << 20) // math.isqrt(standing ** slope) + 1 for standing in range(1, number_of + 1)]
    largest = most if full else min(most, max(-(-total // number_of), total * loads[0] // sum(loads)))
    least = 1 if total - largest >= number_of - 1 else 0
    given, rest = [largest] + [least] * (number_of - 1), total - largest - least * (number_of - 1)
    while rest > 0:
        candidates = [i for i in range(1, number_of) if given[i] < largest] or [i for i in range(1, number_of) if given[i] < most]
        mass, remaining = sum([loads[i] for i in candidates]), rest
        for i in candidates:
            addition = min(most - given[i], max(1, remaining * loads[i] // mass), rest)
            given[i] = given[i] + addition
            rest = rest - addition
    return np.array(given)


def gaussian(rng, extent, width, limit, pieces=(), kind=jnp.bfloat16):
    values = width * jax.random.normal(rng, extent, jnp.float32)
    if pieces:
        values = values * block_levels(rng, extent, pieces, -0.22, 0.18)
    return jnp.clip(values, -limit, limit).astype(kind)


def setup_inputs(seed: int = 0, part: int = 0) -> dict:
    arg_keys = jax.random.split(jax.random.key(seed), 8)
    part_keys = jax.random.split(jax.random.fold_in(arg_keys[7], part), 8)
    hidden = gaussian(part_keys[0], (TOKENS, D), 1.0, 6.0, ((0, 16),))
    norm_gain = jnp.clip(jnp.exp(jax.random.uniform(arg_keys[1], (D,), jnp.float32, math.log(0.25), math.log(4.0))), 0.25, 4.0)
    routes_keys = jax.random.split(jax.random.fold_in(part_keys[2], 1), TOKENS // TOK_DEV)
    routes_turns = jax.random.permutation(jax.random.fold_in(part_keys[2], 3), TOKENS // TOK_DEV)
    routes = jax.vmap(lambda own, number: shared_out(jax.random.fold_in(part_keys[2], 2), own, number, TOK_DEV, EXPERTS, TOP, CAP, 2))(routes_keys, routes_turns).reshape((TOKENS, TOP))
    route_weight = jnp.clip(0.05 + 0.95 * jax.random.uniform(part_keys[3], (TOKENS, TOP), jnp.float32) ** block_levels(part_keys[3], (TOKENS, TOP), ((0, 16),), -0.2, 0.2), 0.05, 1.0)
    w_gate = gaussian(arg_keys[4], (EXPERTS, D, FF), D ** -0.5, 0.125, ((0, 16),))
    w_up = gaussian(arg_keys[5], (EXPERTS, D, FF), D ** -0.5, 0.125, ((0, 16),))
    w_down = gaussian(arg_keys[6], (EXPERTS, FF, D), FF ** -0.5, 0.21875, ((0, 16),))
    return dict(hidden=hidden, norm_gain=norm_gain, routes=routes, route_weight=route_weight, w_gate=w_gate, w_up=w_up, w_down=w_down)


def reference(hidden, norm_gain, routes, route_weight, w_gate, w_up, w_down):
    tokens_all = hidden.shape[0]
    n_src = N_EP
    tok = tokens_all // n_src
    xf = hidden.astype(jnp.float32)
    normed = (xf * lax.rsqrt(lax.optimization_barrier(jnp.mean(xf * xf, axis=-1, keepdims=True)) + 1e-06) * norm_gain).astype(jnp.bfloat16)
    share = route_weight / lax.optimization_barrier(jnp.sum(route_weight, axis=1, keepdims=True))
    flat = routes.reshape(n_src, tok * TOP)
    onehot = (flat[:, :, None] == jnp.arange(EXPERTS, dtype=jnp.int32)[None, None, :]).astype(jnp.int32)
    ranked = jnp.cumsum(onehot, axis=1) - onehot
    slot = lax.optimization_barrier(jnp.sum(ranked * onehot, axis=2)).astype(jnp.int32)
    source = jnp.broadcast_to(jnp.arange(n_src, dtype=jnp.int32)[:, None], (n_src, tok * TOP))
    token = source * tok + (jnp.arange(tok * TOP, dtype=jnp.int32) // TOP)[None, :]
    table = jnp.full((EXPERTS, n_src, CAP), tokens_all, jnp.int32).at[flat, source, slot].set(token.astype(jnp.int32))
    wtable = jnp.zeros((EXPERTS, n_src, CAP), jnp.float32).at[flat, source, slot].set(share.reshape(n_src, tok * TOP))
    padded = jnp.concatenate([normed, jnp.zeros((1, D), jnp.bfloat16)], axis=0)

    def expert_step(total, expert):
        index = table[expert].reshape(-1)
        rows = padded[index]
        gate = jnp.dot(rows, w_gate[expert], preferred_element_type=jnp.float32)
        upper = jnp.dot(rows, w_up[expert], preferred_element_type=jnp.float32)
        units = (jax.nn.silu(gate) * upper).astype(jnp.bfloat16)
        result = jnp.dot(units, w_down[expert], preferred_element_type=jnp.float32).astype(jnp.bfloat16)
        weighted = wtable[expert].reshape(-1)[:, None] * result.astype(jnp.float32)
        total = total.at[index].add(weighted, mode='drop')
        return (total, None)
    total, _ = lax.scan(expert_step, jnp.zeros((tokens_all, D), jnp.float32), jnp.arange(EXPERTS, dtype=jnp.int32))
    return total.astype(jnp.bfloat16)
```

```python
import functools

import jax
import jax.numpy as jnp
from jax import lax
from jax.experimental import pallas as pl
from jax.experimental.pallas import tpu as pltpu
from jax.sharding import PartitionSpec as P


def normalise(hidden, norm_gain):
    xf = hidden.astype(jnp.float32)
    return (xf * lax.rsqrt(jnp.mean(xf * xf, axis=-1, keepdims=True) + 1e-06) * norm_gain).astype(
        jnp.bfloat16
    )


def send_slots(hidden, norm_gain, routes, route_weight, w_gate, w_up, w_down):
    count = lax.axis_size("ep")
    tok = hidden.shape[0]
    width = hidden.shape[1]
    picks = routes.shape[1]
    experts = count * w_gate.shape[0]
    slots = tok * picks * 5 // (4 * experts)
    normed = normalise(hidden, norm_gain)
    share = route_weight / jnp.sum(route_weight, axis=1, keepdims=True)
    flat = routes.reshape(-1)
    onehot = (flat[:, None] == jnp.arange(experts, dtype=jnp.int32)[None, :]).astype(jnp.int32)
    ranked = jnp.cumsum(onehot, axis=0) - onehot
    slot = jnp.sum(ranked * onehot, axis=1)
    token_of = jnp.arange(tok * picks, dtype=jnp.int32) // picks
    outgoing = jnp.zeros((experts, slots, width), jnp.bfloat16).at[flat, slot].set(normed[token_of])
    arrived = lax.all_to_all(outgoing, "ep", split_axis=0, concat_axis=0, tiled=True)
    rows = arrived.reshape(-1, width)
    gate = jnp.dot(rows, w_gate[0], preferred_element_type=jnp.float32)
    upper = jnp.dot(rows, w_up[0], preferred_element_type=jnp.float32)
    units = (jax.nn.silu(gate) * upper).astype(jnp.bfloat16)
    result = jnp.dot(units, w_down[0], preferred_element_type=jnp.float32).astype(jnp.bfloat16)
    coming_back = lax.all_to_all(
        result.reshape(arrived.shape), "ep", split_axis=0, concat_axis=0, tiled=True
    )
    picked = coming_back[flat, slot]
    picked = picked.reshape(tok, picks, width).astype(jnp.float32)
    mixed = jnp.einsum("tk,tkd->td", share, picked)
    return mixed.astype(jnp.bfloat16)


def experts_kernel(slots, tile, place, *refs):
    blocks, refs = refs[: 4 * slots], refs[4 * slots :]
    weights, refs = refs[:6], refs[6:]
    mine, other, rows, tail, total = refs
    tok, width = mine.shape[1], mine.shape[2]
    ff = weights[0].shape[2]
    f32, bf16 = jnp.float32, jnp.bfloat16
    for n in range(slots):
        inner_own, outer_own, inner_other, outer_other = blocks[4 * n : 4 * n + 4]

        def load(own, far):
            rows[0:tok, :] = own[:, :width]
            rows[tok:, :] = far[:, :width]
            tail[0:tok, :] = own[:, width:].astype(f32)
            tail[tok:, :] = far[:, width:].astype(f32)

        @pl.when(place[1] == 1)
        def _():
            load(inner_own, inner_other)

        @pl.when(place[1] == 0)
        def _():
            load(outer_own, outer_other)

        x = rows[...]
        shares = tail[...]
        half = shares.shape[1] // 2
        lane = lax.broadcasted_iota(jnp.int32, shares.shape, 1) % half
        for j in range(2):
            wg, wu, wd = weights[3 * j : 3 * j + 3]
            share = jnp.sum(jnp.where(lane == (place[0] ^ j), shares, 0.0), axis=1, keepdims=True)
            for t in range(ff // tile):
                cols = slice(t * tile, (t + 1) * tile)
                gate = jnp.dot(x, wg[0, :, cols], preferred_element_type=f32)
                upper = jnp.dot(x, wu[0, :, cols], preferred_element_type=f32)
                units = (gate / (1.0 + jnp.exp(-gate)) * upper * share).astype(bf16)
                part = jnp.dot(units, wd[0, cols, :], preferred_element_type=f32)
                if j == 0 and t == 0:
                    total[...] = part
                elif j == 0 or t < ff // tile - 1:
                    total[...] += part
                else:
                    done = (total[...] + part).astype(bf16)
                    mine[n] = done[:tok]
                    other[n] = done[tok:]


def run_experts(place, slots, weights):
    tok, wide = slots[0][0].shape
    _, width, ff = weights[0].shape
    n = len(slots)
    vmem = pl.BlockSpec(memory_space=pltpu.VMEM)
    out = jax.ShapeDtypeStruct((n, tok, width), jnp.bfloat16)
    return pl.pallas_call(
        functools.partial(experts_kernel, n, ff // 3),
        in_specs=[pl.BlockSpec(memory_space=pltpu.SMEM)] + [vmem] * (4 * n + 6),
        out_specs=[vmem] * 2,
        out_shape=[out, out],
        scratch_shapes=[
            pltpu.VMEM((2 * tok, width), jnp.bfloat16),
            pltpu.VMEM((2 * tok, wide - width), jnp.float32),
            pltpu.VMEM((2 * tok, width), jnp.float32),
        ],
        compiler_params=pltpu.CompilerParams(vmem_limit_bytes=20 * 2**20),
        cost_estimate=pl.CostEstimate(
            flops=2 * n * tok * 2 * width * ff * 6,
            bytes_accessed=12 * width * ff,
            transcendentals=4 * n * tok * ff,
        ),
    )(place, *[block for slot in slots for block in slot], *weights)


def gather_rows(hidden, norm_gain, routes, route_weight, w_gate, w_up, w_down):
    count = lax.axis_size("ep")
    experts = count * w_gate.shape[0]
    tok, width = hidden.shape
    f32, bf16 = jnp.float32, jnp.bfloat16
    tie = lambda *arrays: lax.optimization_barrier(arrays)

    def line(x, to):
        moves = [(i, to[i // 4] * 4 + i % 4) for i in range(count) if to[i // 4] is not None]
        return lax.ppermute(x, "ep", moves)

    def cross(x, lines=(0, 1, 2, 3)):
        return lax.ppermute(x, "ep", [(i, i ^ 2) for i in range(count) if i // 4 in lines])

    def other_core(x):
        return lax.ppermute(x, "ep", [(i, i ^ 1) for i in range(count)])

    ends, inner = (0, 3), (1, 2)
    pairs, middle = [1, 0, 3, 2], [None, 2, 1, None]
    outward, inward = [None, 0, 3, None], [1, None, None, 2]

    me = lax.axis_index("ep")
    is_inner = (me // 4 == 1) | (me // 4 == 2)
    place = jnp.stack([me, is_inner]).astype(jnp.int32)

    normed = normalise(hidden, norm_gain)
    share = route_weight / jnp.sum(route_weight, axis=1, keepdims=True)
    names = routes[:, :, None] == jnp.arange(experts, dtype=jnp.int32)[None, None, :]
    dense = jnp.sum(jnp.where(names, share[:, :, None], 0.0), axis=1)
    high = dense.astype(bf16)
    low = (dense - high.astype(f32)).astype(bf16)
    gap = jnp.zeros((tok, 64 - experts), bf16)
    own = jnp.concatenate([normed, high, gap, low, gap], axis=1)

    p1, n2, y0 = line(own, pairs), line(own, middle), cross(own)
    p1, n2 = tie(p1, n2)
    n4, n3 = line(p1, middle), line(n2, outward)
    p1, y0 = tie(p1, y0)
    y1 = cross(p1)
    others = [other_core(w) for w in (w_gate, w_up, w_down)]
    n4, n3 = tie(n4, n3)
    n5 = line(n4, outward)
    n3, n2, y1 = tie(n3, n2, y1)
    yn3, yn2 = cross(n3, ends), cross(n2, inner)
    n4, y1 = tie(n4, y1)
    yn4 = cross(n4, inner)
    n5, yn3, yn2 = tie(n5, yn3, yn2)
    yn5 = cross(n5, ends)

    weights = [
        pltpu.with_memory_space_constraint(w, pltpu.VMEM) for w in (w_gate, w_up, w_down, *others)
    ]
    ma, oa = run_experts(place, [(own, own, y0, y0), (p1, p1, y1, y1)], weights)
    mb, ob = run_experts(place, [(n2, n3, yn2, yn3)], weights)
    mc, oc = run_experts(place, [(n4, n5, yn4, yn5)], weights)

    def add(*parts):
        return sum(p.astype(f32) for p in parts).astype(bf16)

    r4 = add(mc[0], cross(oc[0]))
    r3 = add(mb[0], cross(ob[0]))
    r4 = add(r4, line(r4, inward))
    q4 = line(r4, middle)
    r1 = add(ma[1], cross(oa[1]), q4)
    r3 = add(r3, line(r3, inward))
    return add(ma[0], cross(oa[0]), line(r1, pairs), line(r3, middle))


def solution(mesh):
    in_specs = (
        P(("group", "ep"), None),
        P(),
        P(("group", "ep"), None),
        P(("group", "ep"), None),
        P("ep", None, None),
        P("ep", None, None),
        P("ep", None, None),
    )
    out_specs = P(("group", "ep"), None)

    def body(hidden, norm_gain, routes, route_weight, w_gate, w_up, w_down):
        count, tok, picks = mesh.shape["ep"], hidden.shape[0], routes.shape[1]
        dense = count == 16 and w_gate.shape[0] == 1 and 2 * picks >= count
        plan = gather_rows if dense else send_slots
        return plan(hidden, norm_gain, routes, route_weight, w_gate, w_up, w_down)

    return jax.shard_map(body, mesh=mesh, in_specs=in_specs, out_specs=out_specs, check_vma=False)
```

```python
import functools

import jax
import jax.numpy as jnp
from jax import lax
from jax.experimental import pallas as pl
from jax.experimental.pallas import tpu as pltpu
from jax.sharding import PartitionSpec as P


SMALL = pl.CostEstimate(flops=1, bytes_accessed=1, transcendentals=0)


def normalise(hidden, norm_gain):
    xf = hidden.astype(jnp.float32)
    return (xf * lax.rsqrt(jnp.mean(xf * xf, axis=-1, keepdims=True) + 1e-06) * norm_gain).astype(
        jnp.bfloat16
    )


def send_slots(hidden, norm_gain, routes, route_weight, w_gate, w_up, w_down):
    count = lax.axis_size("ep")
    tok = hidden.shape[0]
    width = hidden.shape[1]
    picks = routes.shape[1]
    experts = count * w_gate.shape[0]
    slots = tok * picks * 5 // (4 * experts)
    normed = normalise(hidden, norm_gain)
    share = route_weight / jnp.sum(route_weight, axis=1, keepdims=True)
    flat = routes.reshape(-1)
    onehot = (flat[:, None] == jnp.arange(experts, dtype=jnp.int32)[None, :]).astype(jnp.int32)
    ranked = jnp.cumsum(onehot, axis=0) - onehot
    slot = jnp.sum(ranked * onehot, axis=1)
    token_of = jnp.arange(tok * picks, dtype=jnp.int32) // picks
    outgoing = jnp.zeros((experts, slots, width), jnp.bfloat16).at[flat, slot].set(normed[token_of])
    arrived = lax.all_to_all(outgoing, "ep", split_axis=0, concat_axis=0, tiled=True)
    rows = arrived.reshape(-1, width)
    gate = jnp.dot(rows, w_gate[0], preferred_element_type=jnp.float32)
    upper = jnp.dot(rows, w_up[0], preferred_element_type=jnp.float32)
    units = (jax.nn.silu(gate) * upper).astype(jnp.bfloat16)
    result = jnp.dot(units, w_down[0], preferred_element_type=jnp.float32).astype(jnp.bfloat16)
    coming_back = lax.all_to_all(
        result.reshape(arrived.shape), "ep", split_axis=0, concat_axis=0, tiled=True
    )
    picked = coming_back[flat, slot]
    picked = picked.reshape(tok, picks, width).astype(jnp.float32)
    mixed = jnp.einsum("tk,tkd->td", share, picked)
    return mixed.astype(jnp.bfloat16)


def prepare_kernel(*refs):
    out, sems = refs[4], refs[9]
    hidden, gain, routes, scores = refs[5:9]
    copies = [pltpu.make_async_copy(refs[n], refs[5 + n], sems.at[n]) for n in range(4)]
    for copy in copies:
        copy.start()
    for copy in copies:
        copy.wait()
    f32, bf16 = jnp.float32, jnp.bfloat16
    tok, width = hidden.shape
    x = hidden[...].astype(f32)
    mean = jnp.mean(x * x, axis=-1, keepdims=True)
    out[:, :width] = (x * lax.rsqrt(mean + 1e-06) * gain[...]).astype(bf16)
    score = scores[...].T
    share = score / jnp.sum(score, axis=1, keepdims=True)
    names = routes[...].T
    pad = out.shape[1] - width
    lane = lax.broadcasted_iota(jnp.int32, (tok, pad), 1)
    expert = lane % (pad // 2)
    dense = jnp.zeros((tok, pad), f32)
    for k in range(names.shape[1]):
        dense += jnp.where(expert == names[:, k : k + 1], share[:, k : k + 1], 0.0)
    high = dense.astype(bf16).astype(f32)
    out[:, width:] = jnp.where(lane < pad // 2, high, dense - high).astype(bf16)


def prepare(hidden, norm_gain, routes, route_weight):
    tok, width = hidden.shape
    arrays = (hidden, norm_gain.reshape(1, width), routes.T, route_weight.T)
    return pl.pallas_call(
        prepare_kernel,
        in_specs=[pl.BlockSpec(memory_space=pltpu.HBM)] * 4,
        out_specs=pl.BlockSpec(memory_space=pltpu.VMEM),
        out_shape=jax.ShapeDtypeStruct((tok, width + 128), jnp.bfloat16),
        scratch_shapes=[pltpu.VMEM(array.shape, array.dtype) for array in arrays]
        + [pltpu.SemaphoreType.DMA((4,))],
        compiler_params=pltpu.CompilerParams(vmem_limit_bytes=62 * 2**20),
    )(*arrays)


def hold_kernel(count, *refs):
    token, sems = refs[-2:]
    copies = [pltpu.make_async_copy(refs[n], refs[count + n], sems.at[n]) for n in range(count)]
    for copy in copies:
        copy.start()
    token[...] = jnp.zeros(token.shape, token.dtype)
    for copy in copies:
        copy.wait()


def hold(*arrays):
    count = len(arrays)
    *held, token = pl.pallas_call(
        functools.partial(hold_kernel, count),
        in_specs=[pl.BlockSpec(memory_space=pl.ANY)] * count,
        out_specs=[pl.BlockSpec(memory_space=pltpu.VMEM)] * (count + 1),
        out_shape=[pltpu.VMEM(array.shape, array.dtype) for array in arrays]
        + [jax.ShapeDtypeStruct((8, 128), jnp.float32)],
        scratch_shapes=[pltpu.SemaphoreType.DMA((count,))],
        compiler_params=pltpu.CompilerParams(vmem_limit_bytes=2 * 2**20),
        cost_estimate=SMALL,
    )(*[pltpu.with_memory_space_constraint(array, pltpu.HBM) for array in arrays])
    return held, token


def again_kernel(array, after, out, sem):
    del after
    copy = pltpu.make_async_copy(array, out, sem)
    copy.start()
    copy.wait()


def again(array, after):
    anywhere = pl.BlockSpec(memory_space=pl.ANY)
    return pl.pallas_call(
        again_kernel,
        in_specs=[anywhere] * 2,
        out_specs=anywhere,
        out_shape=jax.ShapeDtypeStruct(array.shape, array.dtype),
        scratch_shapes=[pltpu.SemaphoreType.DMA],
        compiler_params=pltpu.CompilerParams(vmem_limit_bytes=2**20),
        cost_estimate=SMALL,
    )(pltpu.with_memory_space_constraint(array, pltpu.HBM), after)


def gate_kernel(*refs):
    del refs


def gate(through, after):
    count = len(through)
    anywhere = pl.BlockSpec(memory_space=pl.ANY)
    return pl.pallas_call(
        gate_kernel,
        in_specs=[anywhere] * (count + len(after)),
        out_specs=[anywhere] * count,
        out_shape=[jax.ShapeDtypeStruct(array.shape, array.dtype) for array in through],
        input_output_aliases={n: n for n in range(count)},
        compiler_params=pltpu.CompilerParams(vmem_limit_bytes=2**20),
        cost_estimate=SMALL,
    )(*through, *after)


def experts_kernel(pieces, tile, *refs):
    me = lax.axis_index("ep")
    line = me // 4
    is_inner = (line == 1) | (line == 2)
    blocks = []
    for count in pieces:
        blocks.append(refs[:count])
        refs = refs[count:]
    weights, refs = refs[:6], refs[6:]
    outs, refs = refs[: len(pieces)], refs[len(pieces) :]
    rows, total, sems = refs
    width = outs[0].shape[1]
    ff = weights[0].shape[2]
    f32, bf16 = jnp.float32, jnp.bfloat16

    def each_block(act):
        at = 0
        for p, block in enumerate(blocks):
            size = block[0].shape[0]
            for n, ref in enumerate(block):
                copy = pltpu.make_async_copy(ref, rows.at[pl.ds(at, size)], sems.at[p, n])
                if len(block) == 1:
                    act(copy)
                else:
                    pl.when(is_inner if n == 0 else ~is_inner)(functools.partial(act, copy))
            at += size

    each_block(lambda copy: copy.start())
    each_block(lambda copy: copy.wait())

    shares = rows[:, width:].astype(f32)
    half = shares.shape[1] // 2
    lane = lax.broadcasted_iota(jnp.int32, shares.shape, 1) % half
    x = rows[:, :width]
    steps = ff // tile
    for j in range(2):
        wg, wu, wd = weights[3 * j : 3 * j + 3]
        share = jnp.sum(jnp.where(lane == (me ^ j), shares, 0.0), axis=1, keepdims=True)
        for t in range(steps):
            some = pl.ds(t * tile, tile)
            gate = jnp.dot(x, wg[0, :, some], preferred_element_type=f32)
            upper = jnp.dot(x, wu[0, :, some], preferred_element_type=f32)
            units = (gate / (1.0 + jnp.exp(-gate)) * upper * share).astype(bf16)
            part = jnp.dot(units, wd[0, some, :], preferred_element_type=f32)
            if j == 0 and t == 0:
                total[...] = part
            elif j == 0 or t < steps - 1:
                total[...] += part
            else:
                done = (total[...] + part).astype(bf16)
                at = 0
                for out in outs:
                    out[...] = done[at : at + out.shape[0]]
                    at += out.shape[0]


def run_experts(pieces, weights):
    sizes = [piece[0].shape[0] for piece in pieces]
    wide = pieces[0][0].shape[1]
    _, width, ff = weights[0].shape
    whole = sum(sizes)
    blocks = [block for piece in pieces for block in piece]
    vmem, anywhere = pl.BlockSpec(memory_space=pltpu.VMEM), pl.BlockSpec(memory_space=pl.ANY)
    return pl.pallas_call(
        functools.partial(experts_kernel, [len(piece) for piece in pieces], ff // 3),
        in_specs=[anywhere] * len(blocks) + [vmem] * 6,
        out_specs=[vmem] * len(pieces),
        out_shape=[jax.ShapeDtypeStruct((size, width), jnp.bfloat16) for size in sizes],
        scratch_shapes=[
            pltpu.VMEM((whole, wide), jnp.bfloat16),
            pltpu.VMEM((whole, width), jnp.float32),
            pltpu.SemaphoreType.DMA((len(pieces), 2)),
        ],
        compiler_params=pltpu.CompilerParams(vmem_limit_bytes=20 * 2**20),
        cost_estimate=SMALL,
    )(*blocks, *weights)


def gather_rows(hidden, norm_gain, routes, route_weight, w_gate, w_up, w_down):
    count = lax.axis_size("ep")
    f32, bf16 = jnp.float32, jnp.bfloat16
    tie = lambda *arrays: lax.optimization_barrier(arrays)

    def line(x, to):
        moves = [(i, to[i // 4] * 4 + i % 4) for i in range(count) if to[i // 4] is not None]
        return lax.ppermute(x, "ep", moves)

    def cross(x, lines=(0, 1, 2, 3)):
        return lax.ppermute(x, "ep", [(i, i ^ 2) for i in range(count) if i // 4 in lines])

    def other_core(x):
        return lax.ppermute(x, "ep", [(i, i ^ 1) for i in range(count)])

    ends, inner = (0, 3), (1, 2)
    pairs, middle = [1, 0, 3, 2], [None, 2, 1, None]
    outward, inward = [None, 0, 3, None], [1, None, None, 2]

    far_gate, far_up = other_core(w_gate), other_core(w_up)
    own = prepare(hidden, norm_gain, routes, route_weight)

    p1, n2, y0 = line(own, pairs), line(own, middle), cross(own)
    weights, token = hold(w_gate, w_up, w_down)
    p1, n2, y0, far_gate, far_up = gate([p1, n2, y0, far_gate, far_up], [token])

    n4, n3, yn2 = line(p1, middle), line(n2, outward), cross(n2, inner)
    far_down = other_core(again(w_down, p1))
    held, token = hold(far_gate, far_up)
    weights += held
    n4, n3, yn2, far_down = gate([n4, n3, yn2, far_down], [token])

    n5, yn3, yn4 = line(n4, outward), cross(n3, ends), cross(n4, inner)
    held, token = hold(far_down)
    weights += held
    m0, o0 = run_experts([(own,), (y0,)], weights)
    n5, yn3, yn4 = gate([n5, yn3, yn4], [o0])

    yn5, y1 = cross(n5, ends), line(y0, pairs)
    m3, o3 = run_experts([(n2, n3), (yn2, yn3)], weights)
    yn5, y1 = gate([yn5, y1], [o3])
    m4, o4 = run_experts([(n4, n5), (yn4, yn5)], weights)

    def add(*parts):
        return sum(p.astype(f32) for p in parts).astype(bf16)

    o4 = cross(o4)
    m1, o1 = run_experts([(p1,), (y1,)], weights)
    o4, o3 = gate([o4, o3], [o1])
    r4 = add(m4, o4)
    r3 = add(m3, cross(o3))
    r4 = add(r4, line(r4, inward))
    r1 = add(m1, cross(o1), line(r4, middle))
    r3 = add(r3, line(r3, inward))
    return add(m0, cross(o0), line(r1, pairs), line(r3, middle))


def solution(mesh):
    in_specs = (
        P(("group", "ep"), None),
        P(),
        P(("group", "ep"), None),
        P(("group", "ep"), None),
        P("ep", None, None),
        P("ep", None, None),
        P("ep", None, None),
    )
    out_specs = P(("group", "ep"), None)

    def body(hidden, norm_gain, routes, route_weight, w_gate, w_up, w_down):
        count, tok, picks = mesh.shape["ep"], hidden.shape[0], routes.shape[1]
        dense = count == 16 and w_gate.shape[0] == 1 and 2 * picks >= count
        plan = gather_rows if dense else send_slots
        return plan(hidden, norm_gain, routes, route_weight, w_gate, w_up, w_down)

    return jax.shard_map(body, mesh=mesh, in_specs=in_specs, out_specs=out_specs, check_vma=False)
```

```python
import functools

import jax
import jax.numpy as jnp
from jax import lax
from jax.experimental import pallas as pl
from jax.experimental.pallas import tpu as pltpu
from jax.sharding import PartitionSpec as P


SMALL = pl.CostEstimate(flops=1, bytes_accessed=1, transcendentals=0)


def normalise(hidden, norm_gain):
    xf = hidden.astype(jnp.float32)
    return (xf * lax.rsqrt(jnp.mean(xf * xf, axis=-1, keepdims=True) + 1e-06) * norm_gain).astype(
        jnp.bfloat16
    )


def send_slots(hidden, norm_gain, routes, route_weight, w_gate, w_up, w_down):
    count = lax.axis_size("ep")
    tok = hidden.shape[0]
    width = hidden.shape[1]
    picks = routes.shape[1]
    experts = count * w_gate.shape[0]
    slots = tok * picks * 5 // (4 * experts)
    normed = normalise(hidden, norm_gain)
    share = route_weight / jnp.sum(route_weight, axis=1, keepdims=True)
    flat = routes.reshape(-1)
    onehot = (flat[:, None] == jnp.arange(experts, dtype=jnp.int32)[None, :]).astype(jnp.int32)
    ranked = jnp.cumsum(onehot, axis=0) - onehot
    slot = jnp.sum(ranked * onehot, axis=1)
    token_of = jnp.arange(tok * picks, dtype=jnp.int32) // picks
    outgoing = jnp.zeros((experts, slots, width), jnp.bfloat16).at[flat, slot].set(normed[token_of])
    arrived = lax.all_to_all(outgoing, "ep", split_axis=0, concat_axis=0, tiled=True)
    rows = arrived.reshape(-1, width)
    gate = jnp.dot(rows, w_gate[0], preferred_element_type=jnp.float32)
    upper = jnp.dot(rows, w_up[0], preferred_element_type=jnp.float32)
    units = (jax.nn.silu(gate) * upper).astype(jnp.bfloat16)
    result = jnp.dot(units, w_down[0], preferred_element_type=jnp.float32).astype(jnp.bfloat16)
    coming_back = lax.all_to_all(
        result.reshape(arrived.shape), "ep", split_axis=0, concat_axis=0, tiled=True
    )
    picked = coming_back[flat, slot]
    picked = picked.reshape(tok, picks, width).astype(jnp.float32)
    mixed = jnp.einsum("tk,tkd->td", share, picked)
    return mixed.astype(jnp.bfloat16)


def prepare_kernel(*refs):
    out, sems = refs[4], refs[9]
    hidden, gain, routes, scores = refs[5:9]
    copies = [pltpu.make_async_copy(refs[n], refs[5 + n], sems.at[n]) for n in range(4)]
    for copy in copies:
        copy.start()
    for copy in copies:
        copy.wait()
    f32, bf16 = jnp.float32, jnp.bfloat16
    tok, width = hidden.shape
    x = hidden[...].astype(f32)
    mean = jnp.mean(x * x, axis=-1, keepdims=True)
    out[:, :width] = (x * lax.rsqrt(mean + 1e-06) * gain[...]).astype(bf16)
    score = scores[...].T
    share = score / jnp.sum(score, axis=1, keepdims=True)
    names = routes[...].T
    pad = out.shape[1] - width
    lane = lax.broadcasted_iota(jnp.int32, (tok, pad), 1)
    expert = lane % (pad // 2)
    dense = jnp.zeros((tok, pad), f32)
    for k in range(names.shape[1]):
        dense += jnp.where(expert == names[:, k : k + 1], share[:, k : k + 1], 0.0)
    high = dense.astype(bf16).astype(f32)
    out[:, width:] = jnp.where(lane < pad // 2, high, dense - high).astype(bf16)


def prepare(hidden, norm_gain, routes, route_weight):
    tok, width = hidden.shape
    arrays = (hidden, norm_gain.reshape(1, width), routes.T, route_weight.T)
    return pl.pallas_call(
        prepare_kernel,
        in_specs=[pl.BlockSpec(memory_space=pltpu.HBM)] * 4,
        out_specs=pl.BlockSpec(memory_space=pltpu.VMEM),
        out_shape=jax.ShapeDtypeStruct((tok, width + 128), jnp.bfloat16),
        scratch_shapes=[pltpu.VMEM(array.shape, array.dtype) for array in arrays]
        + [pltpu.SemaphoreType.DMA((4,))],
        compiler_params=pltpu.CompilerParams(vmem_limit_bytes=62 * 2**20),
    )(*arrays)


def hold_kernel(count, *refs):
    token, sems = refs[-2:]
    copies = [pltpu.make_async_copy(refs[n], refs[count + n], sems.at[n]) for n in range(count)]
    for copy in copies:
        copy.start()
    token[...] = jnp.zeros(token.shape, token.dtype)
    for copy in copies:
        copy.wait()


def hold(*arrays):
    count = len(arrays)
    *held, token = pl.pallas_call(
        functools.partial(hold_kernel, count),
        in_specs=[pl.BlockSpec(memory_space=pl.ANY)] * count,
        out_specs=[pl.BlockSpec(memory_space=pltpu.VMEM)] * (count + 1),
        out_shape=[pltpu.VMEM(array.shape, array.dtype) for array in arrays]
        + [jax.ShapeDtypeStruct((8, 128), jnp.float32)],
        scratch_shapes=[pltpu.SemaphoreType.DMA((count,))],
        compiler_params=pltpu.CompilerParams(vmem_limit_bytes=2 * 2**20),
        cost_estimate=SMALL,
    )(*[pltpu.with_memory_space_constraint(array, pltpu.HBM) for array in arrays])
    return held, token


def again_kernel(array, after, out, sem):
    del after
    copy = pltpu.make_async_copy(array, out, sem)
    copy.start()
    copy.wait()


def again(array, after):
    anywhere = pl.BlockSpec(memory_space=pl.ANY)
    return pl.pallas_call(
        again_kernel,
        in_specs=[anywhere] * 2,
        out_specs=anywhere,
        out_shape=jax.ShapeDtypeStruct(array.shape, array.dtype),
        scratch_shapes=[pltpu.SemaphoreType.DMA],
        compiler_params=pltpu.CompilerParams(vmem_limit_bytes=2**20),
        cost_estimate=SMALL,
    )(pltpu.with_memory_space_constraint(array, pltpu.HBM), after)


def gate_kernel(*refs):
    del refs


def gate(through, after):
    count = len(through)
    anywhere = pl.BlockSpec(memory_space=pl.ANY)
    return pl.pallas_call(
        gate_kernel,
        in_specs=[anywhere] * (count + len(after)),
        out_specs=[anywhere] * count,
        out_shape=[jax.ShapeDtypeStruct(array.shape, array.dtype) for array in through],
        input_output_aliases={n: n for n in range(count)},
        compiler_params=pltpu.CompilerParams(vmem_limit_bytes=2**20),
        cost_estimate=SMALL,
    )(*through, *after)


def experts_kernel(count, tile, *refs):
    me = lax.axis_index("ep")
    blocks, weights, outs = refs[:count], refs[count : count + 6], refs[count + 6 : 2 * count + 6]
    rows, total, sems = refs[2 * count + 6 :]
    width = outs[0].shape[1]
    ff = weights[0].shape[2]
    f32, bf16 = jnp.float32, jnp.bfloat16

    copies, at = [], 0
    for n, block in enumerate(blocks):
        size = block.shape[0]
        copies.append(pltpu.make_async_copy(block, rows.at[pl.ds(at, size)], sems.at[n]))
        at += size
    for copy in copies:
        copy.start()
    for copy in copies:
        copy.wait()

    shares = rows[:, width:].astype(f32)
    half = shares.shape[1] // 2
    lane = lax.broadcasted_iota(jnp.int32, shares.shape, 1) % half
    x = rows[:, :width]
    steps = ff // tile
    for j in range(2):
        wg, wu, wd = weights[3 * j : 3 * j + 3]
        share = jnp.sum(jnp.where(lane == (me ^ j), shares, 0.0), axis=1, keepdims=True)
        for t in range(steps):
            some = pl.ds(t * tile, tile)
            gate = jnp.dot(x, wg[0, :, some], preferred_element_type=f32)
            upper = jnp.dot(x, wu[0, :, some], preferred_element_type=f32)
            units = (gate / (1.0 + jnp.exp(-gate)) * upper * share).astype(bf16)
            part = jnp.dot(units, wd[0, some, :], preferred_element_type=f32)
            if j == 0 and t == 0:
                total[...] = part
            elif j == 0 or t < steps - 1:
                total[...] += part
            else:
                done = (total[...] + part).astype(bf16)
                at = 0
                for out in outs:
                    out[...] = done[at : at + out.shape[0]]
                    at += out.shape[0]


def run_experts(blocks, weights):
    count = len(blocks)
    sizes = [block.shape[0] for block in blocks]
    wide = blocks[0].shape[1]
    _, width, ff = weights[0].shape
    whole = sum(sizes)
    vmem, anywhere = pl.BlockSpec(memory_space=pltpu.VMEM), pl.BlockSpec(memory_space=pl.ANY)
    return pl.pallas_call(
        functools.partial(experts_kernel, count, ff // 3),
        in_specs=[anywhere] * count + [vmem] * 6,
        out_specs=[vmem] * count,
        out_shape=[jax.ShapeDtypeStruct((size, width), jnp.bfloat16) for size in sizes],
        scratch_shapes=[
            pltpu.VMEM((whole, wide), jnp.bfloat16),
            pltpu.VMEM((whole, width), jnp.float32),
            pltpu.SemaphoreType.DMA((count,)),
        ],
        compiler_params=pltpu.CompilerParams(vmem_limit_bytes=20 * 2**20),
        cost_estimate=SMALL,
    )(*blocks, *weights)


def choose_kernel(inner, outer, out, sem):
    line = lax.axis_index("ep") // 4
    is_inner = (line == 1) | (line == 2)

    def take(array):
        copy = pltpu.make_async_copy(array, out, sem)
        copy.start()
        copy.wait()

    pl.when(is_inner)(functools.partial(take, inner))
    pl.when(~is_inner)(functools.partial(take, outer))


def choose(inner, outer):
    anywhere = pl.BlockSpec(memory_space=pl.ANY)
    return pl.pallas_call(
        choose_kernel,
        in_specs=[anywhere] * 2,
        out_specs=anywhere,
        out_shape=jax.ShapeDtypeStruct(inner.shape, inner.dtype),
        scratch_shapes=[pltpu.SemaphoreType.DMA],
        compiler_params=pltpu.CompilerParams(vmem_limit_bytes=2**20),
        cost_estimate=SMALL,
    )(inner, outer)


def gather_rows(hidden, norm_gain, routes, route_weight, w_gate, w_up, w_down):
    count = lax.axis_size("ep")
    f32, bf16 = jnp.float32, jnp.bfloat16
    tie = lambda *arrays: lax.optimization_barrier(arrays)

    def line(x, to):
        moves = [(i, to[i // 4] * 4 + i % 4) for i in range(count) if to[i // 4] is not None]
        return lax.ppermute(x, "ep", moves)

    def cross(x):
        return lax.ppermute(x, "ep", [(i, i ^ 2) for i in range(count)])

    def other_core(x):
        return lax.ppermute(x, "ep", [(i, i ^ 1) for i in range(count)])

    def add(*parts):
        return sum(p.astype(f32) for p in parts).astype(bf16)

    far, back = [2, 0, 3, 1], [1, 3, 0, 2]
    pairs, middle = [1, 0, 3, 2], [None, 2, 1, None]
    outward, inward = [None, 0, 3, None], [1, None, None, 2]

    far_gate, far_up = other_core(w_gate), other_core(w_up)
    own = prepare(hidden, norm_gain, routes, route_weight)

    a, y0 = line(own, far), cross(own)
    weights, token = hold(w_gate, w_up, w_down)
    a, y0, far_gate, far_up = gate([a, y0, far_gate, far_up], [token])

    b, n, ya = line(choose(a, own), pairs), line(own, middle), cross(a)
    far_down = other_core(w_down)
    held, token = hold(far_gate, far_up)
    weights += held
    b, n, ya = gate([b, n, ya], [token])

    c, yb = line(n, outward), cross(b)
    held, token = hold(far_down)
    weights += held
    m0, o0 = run_experts([own, y0], weights)
    c, yb = gate([c, yb], [o0])

    c = choose(n, c)
    yc = cross(c)
    ma, oa = run_experts([a, ya], weights)
    (yc,) = gate([yc], [oa])
    mc, oc = run_experts([c, yc], weights)

    oc = cross(oc)
    mb, ob = run_experts([b, yb], weights)
    oc, ob = gate([oc, ob], [])
    rc = add(mc, oc)
    rb = add(mb, cross(ob))
    rc = add(rc, line(rc, inward))
    p = line(rb, pairs)
    place = lax.axis_index("ep") // 4
    is_inner = (place == 1) | (place == 2)
    zero = jnp.zeros_like(p)
    ra = add(ma, cross(oa), jnp.where(is_inner, p, zero))
    return add(m0, cross(o0), line(ra, back), line(rc, middle), jnp.where(is_inner, zero, p))


def solution(mesh):
    in_specs = (
        P(("group", "ep"), None),
        P(),
        P(("group", "ep"), None),
        P(("group", "ep"), None),
        P("ep", None, None),
        P("ep", None, None),
        P("ep", None, None),
    )
    out_specs = P(("group", "ep"), None)

    def body(hidden, norm_gain, routes, route_weight, w_gate, w_up, w_down):
        count, tok, picks = mesh.shape["ep"], hidden.shape[0], routes.shape[1]
        dense = count == 16 and w_gate.shape[0] == 1 and 2 * picks >= count
        plan = gather_rows if dense else send_slots
        return plan(hidden, norm_gain, routes, route_weight, w_gate, w_up, w_down)

    return jax.shard_map(body, mesh=mesh, in_specs=in_specs, out_specs=out_specs, check_vma=False)
```

```python
import functools

import jax
import jax.numpy as jnp
from jax import lax
from jax.experimental import pallas as pl
from jax.experimental.pallas import tpu as pltpu
from jax.sharding import PartitionSpec as P


SMALL = pl.CostEstimate(flops=1, bytes_accessed=1, transcendentals=0)


def normalise(hidden, norm_gain):
    xf = hidden.astype(jnp.float32)
    return (xf * lax.rsqrt(jnp.mean(xf * xf, axis=-1, keepdims=True) + 1e-06) * norm_gain).astype(
        jnp.bfloat16
    )


def send_slots(hidden, norm_gain, routes, route_weight, w_gate, w_up, w_down):
    count = lax.axis_size("ep")
    tok = hidden.shape[0]
    width = hidden.shape[1]
    picks = routes.shape[1]
    experts = count * w_gate.shape[0]
    slots = tok * picks * 5 // (4 * experts)
    normed = normalise(hidden, norm_gain)
    share = route_weight / jnp.sum(route_weight, axis=1, keepdims=True)
    flat = routes.reshape(-1)
    onehot = (flat[:, None] == jnp.arange(experts, dtype=jnp.int32)[None, :]).astype(jnp.int32)
    ranked = jnp.cumsum(onehot, axis=0) - onehot
    slot = jnp.sum(ranked * onehot, axis=1)
    token_of = jnp.arange(tok * picks, dtype=jnp.int32) // picks
    outgoing = jnp.zeros((experts, slots, width), jnp.bfloat16).at[flat, slot].set(normed[token_of])
    arrived = lax.all_to_all(outgoing, "ep", split_axis=0, concat_axis=0, tiled=True)
    rows = arrived.reshape(-1, width)
    gate = jnp.dot(rows, w_gate[0], preferred_element_type=jnp.float32)
    upper = jnp.dot(rows, w_up[0], preferred_element_type=jnp.float32)
    units = (jax.nn.silu(gate) * upper).astype(jnp.bfloat16)
    result = jnp.dot(units, w_down[0], preferred_element_type=jnp.float32).astype(jnp.bfloat16)
    coming_back = lax.all_to_all(
        result.reshape(arrived.shape), "ep", split_axis=0, concat_axis=0, tiled=True
    )
    picked = coming_back[flat, slot]
    picked = picked.reshape(tok, picks, width).astype(jnp.float32)
    mixed = jnp.einsum("tk,tkd->td", share, picked)
    return mixed.astype(jnp.bfloat16)


def prepare_kernel(*refs):
    out, sems = refs[4], refs[9]
    hidden, gain, routes, scores = refs[5:9]
    copies = [pltpu.make_async_copy(refs[n], refs[5 + n], sems.at[n]) for n in range(4)]
    for copy in copies:
        copy.start()
    for copy in copies:
        copy.wait()
    f32, bf16 = jnp.float32, jnp.bfloat16
    tok, width = hidden.shape
    x = hidden[...].astype(f32)
    mean = jnp.mean(x * x, axis=-1, keepdims=True)
    out[:, :width] = (x * lax.rsqrt(mean + 1e-06) * gain[...]).astype(bf16)
    score = scores[...].T
    share = score / jnp.sum(score, axis=1, keepdims=True)
    names = routes[...].T
    pad = out.shape[1] - width
    lane = lax.broadcasted_iota(jnp.int32, (tok, pad), 1)
    expert = lane % (pad // 2)
    dense = jnp.zeros((tok, pad), f32)
    for k in range(names.shape[1]):
        dense += jnp.where(expert == names[:, k : k + 1], share[:, k : k + 1], 0.0)
    high = dense.astype(bf16).astype(f32)
    out[:, width:] = jnp.where(lane < pad // 2, high, dense - high).astype(bf16)


def prepare(hidden, norm_gain, routes, route_weight):
    tok, width = hidden.shape
    arrays = (hidden, norm_gain.reshape(1, width), routes.T, route_weight.T)
    return pl.pallas_call(
        prepare_kernel,
        in_specs=[pl.BlockSpec(memory_space=pltpu.HBM)] * 4,
        out_specs=pl.BlockSpec(memory_space=pltpu.VMEM),
        out_shape=jax.ShapeDtypeStruct((tok, width + 128), jnp.bfloat16),
        scratch_shapes=[pltpu.VMEM(array.shape, array.dtype) for array in arrays]
        + [pltpu.SemaphoreType.DMA((4,))],
        compiler_params=pltpu.CompilerParams(vmem_limit_bytes=62 * 2**20),
    )(*arrays)


def hold_kernel(count, *refs):
    token, sems = refs[-2:]
    copies = [pltpu.make_async_copy(refs[n], refs[count + n], sems.at[n]) for n in range(count)]
    for copy in copies:
        copy.start()
    token[...] = jnp.zeros(token.shape, token.dtype)
    for copy in copies:
        copy.wait()


def hold(*arrays):
    count = len(arrays)
    *held, token = pl.pallas_call(
        functools.partial(hold_kernel, count),
        in_specs=[pl.BlockSpec(memory_space=pl.ANY)] * count,
        out_specs=[pl.BlockSpec(memory_space=pltpu.VMEM)] * (count + 1),
        out_shape=[pltpu.VMEM(array.shape, array.dtype) for array in arrays]
        + [jax.ShapeDtypeStruct((8, 128), jnp.float32)],
        scratch_shapes=[pltpu.SemaphoreType.DMA((count,))],
        compiler_params=pltpu.CompilerParams(vmem_limit_bytes=2 * 2**20),
        cost_estimate=SMALL,
    )(*[pltpu.with_memory_space_constraint(array, pltpu.HBM) for array in arrays])
    return held, token


def again_kernel(array, after, out, sem):
    del after
    copy = pltpu.make_async_copy(array, out, sem)
    copy.start()
    copy.wait()


def again(array, after):
    anywhere = pl.BlockSpec(memory_space=pl.ANY)
    return pl.pallas_call(
        again_kernel,
        in_specs=[anywhere] * 2,
        out_specs=anywhere,
        out_shape=jax.ShapeDtypeStruct(array.shape, array.dtype),
        scratch_shapes=[pltpu.SemaphoreType.DMA],
        compiler_params=pltpu.CompilerParams(vmem_limit_bytes=2**20),
        cost_estimate=SMALL,
    )(pltpu.with_memory_space_constraint(array, pltpu.HBM), after)


def gate_kernel(*refs):
    del refs


def gate(through, after):
    count = len(through)
    anywhere = pl.BlockSpec(memory_space=pl.ANY)
    return pl.pallas_call(
        gate_kernel,
        in_specs=[anywhere] * (count + len(after)),
        out_specs=[anywhere] * count,
        out_shape=[jax.ShapeDtypeStruct(array.shape, array.dtype) for array in through],
        input_output_aliases={n: n for n in range(count)},
        compiler_params=pltpu.CompilerParams(vmem_limit_bytes=2**20),
        cost_estimate=SMALL,
    )(*through, *after)


def experts_kernel(count, tile, *refs):
    me = lax.axis_index("ep")
    blocks, weights, outs = refs[:count], refs[count : count + 6], refs[count + 6 : 2 * count + 6]
    rows, total, sems = refs[2 * count + 6 :]
    width = outs[0].shape[1]
    ff = weights[0].shape[2]
    f32, bf16 = jnp.float32, jnp.bfloat16

    copies, at = [], 0
    for n, block in enumerate(blocks):
        size = block.shape[0]
        copies.append(pltpu.make_async_copy(block, rows.at[pl.ds(at, size)], sems.at[n]))
        at += size
    for copy in copies:
        copy.start()
    for copy in copies:
        copy.wait()

    shares = rows[:, width:].astype(f32)
    half = shares.shape[1] // 2
    lane = lax.broadcasted_iota(jnp.int32, shares.shape, 1) % half
    x = rows[:, :width]
    steps = ff // tile
    for j in range(2):
        wg, wu, wd = weights[3 * j : 3 * j + 3]
        share = jnp.sum(jnp.where(lane == (me ^ j), shares, 0.0), axis=1, keepdims=True)
        for t in range(steps):
            some = pl.ds(t * tile, tile)
            gate = jnp.dot(x, wg[0, :, some], preferred_element_type=f32)
            upper = jnp.dot(x, wu[0, :, some], preferred_element_type=f32)
            units = (gate / (1.0 + jnp.exp(-gate)) * upper * share).astype(bf16)
            part = jnp.dot(units, wd[0, some, :], preferred_element_type=f32)
            if j == 0 and t == 0:
                total[...] = part
            elif j == 0 or t < steps - 1:
                total[...] += part
            else:
                done = (total[...] + part).astype(bf16)
                at = 0
                for out in outs:
                    out[...] = done[at : at + out.shape[0]]
                    at += out.shape[0]


def run_experts(blocks, weights):
    count = len(blocks)
    sizes = [block.shape[0] for block in blocks]
    wide = blocks[0].shape[1]
    _, width, ff = weights[0].shape
    whole = sum(sizes)
    vmem, anywhere = pl.BlockSpec(memory_space=pltpu.VMEM), pl.BlockSpec(memory_space=pl.ANY)
    return pl.pallas_call(
        functools.partial(experts_kernel, count, ff // 3),
        in_specs=[anywhere] * count + [vmem] * 6,
        out_specs=[vmem] * count,
        out_shape=[jax.ShapeDtypeStruct((size, width), jnp.bfloat16) for size in sizes],
        scratch_shapes=[
            pltpu.VMEM((whole, wide), jnp.bfloat16),
            pltpu.VMEM((whole, width), jnp.float32),
            pltpu.SemaphoreType.DMA((count,)),
        ],
        compiler_params=pltpu.CompilerParams(vmem_limit_bytes=20 * 2**20),
        cost_estimate=SMALL,
    )(*blocks, *weights)


def choose_kernel(inner, outer, out, sem):
    line = lax.axis_index("ep") // 4
    is_inner = (line == 1) | (line == 2)

    def take(array):
        copy = pltpu.make_async_copy(array, out, sem)
        copy.start()
        copy.wait()

    pl.when(is_inner)(functools.partial(take, inner))
    pl.when(~is_inner)(functools.partial(take, outer))


def choose(inner, outer):
    anywhere = pl.BlockSpec(memory_space=pl.ANY)
    return pl.pallas_call(
        choose_kernel,
        in_specs=[anywhere] * 2,
        out_specs=anywhere,
        out_shape=jax.ShapeDtypeStruct(inner.shape, inner.dtype),
        scratch_shapes=[pltpu.SemaphoreType.DMA],
        compiler_params=pltpu.CompilerParams(vmem_limit_bytes=2**20),
        cost_estimate=SMALL,
    )(inner, outer)


def gather_rows(hidden, norm_gain, routes, route_weight, w_gate, w_up, w_down):
    count = lax.axis_size("ep")
    f32, bf16 = jnp.float32, jnp.bfloat16
    tie = lambda *arrays: lax.optimization_barrier(arrays)

    def line(x, to):
        moves = [(i, to[i // 4] * 4 + i % 4) for i in range(count) if to[i // 4] is not None]
        return lax.ppermute(x, "ep", moves)

    def cross(x):
        return lax.ppermute(x, "ep", [(i, i ^ 2) for i in range(count)])

    def other_core(x):
        return lax.ppermute(x, "ep", [(i, i ^ 1) for i in range(count)])

    def add(*parts):
        return sum(p.astype(f32) for p in parts).astype(bf16)

    far, back = [2, 0, 3, 1], [1, 3, 0, 2]
    pairs, middle = [1, 0, 3, 2], [None, 2, 1, None]
    outward, inward = [None, 0, 3, None], [1, None, None, 2]
    far_ends = [None, 3, 0, None]

    far_gate, far_up = other_core(w_gate), other_core(w_up)
    own = prepare(hidden, norm_gain, routes, route_weight)

    a, y0 = line(own, far), cross(own)
    weights, token = hold(w_gate, w_up, w_down)
    a, y0, far_gate, far_up = gate([a, y0, far_gate, far_up], [token])

    b, n, ya = line(choose(a, own), pairs), line(own, middle), cross(a)
    far_down = other_core(w_down)
    held, token = hold(far_gate, far_up)
    weights += held
    b, n, ya = gate([b, n, ya], [token])

    c, yb = line(n, outward), cross(b)
    held, token = hold(far_down)
    weights += held
    m0, o0 = run_experts([own, y0], weights)
    c, yb = gate([c, yb], [o0])

    c = choose(n, c)
    yc = cross(c)
    ma, oa = run_experts([a, ya], weights)
    mb, ob = run_experts([b, yb], weights)
    yc, ob = gate([yc, ob], [oa])

    place = lax.axis_index("ep") // 4
    is_inner = (place == 1) | (place == 2)

    yob, xo = cross(ob), line(oa, back)
    mc, oc = run_experts([c, yc], weights)
    yob, xo, oc = gate([yob, xo, oc], [])

    yoc, p = cross(oc), line(add(mb, yob), pairs)
    o0 = add(o0, xo)
    yoc, p, o0 = gate([yoc, p, o0], [])

    yo0 = cross(o0)
    rc = add(mc, yoc)
    q, xm = line(rc, inward), line(add(ma, p), far_ends)
    m0 = add(m0, jnp.where(is_inner, jnp.zeros_like(p), p))
    yo0, q, xm, ma, m0 = gate([yo0, q, xm, ma, m0], [])

    xe, xn = line(ma, inward), line(add(rc, q), middle)
    return add(m0, yo0, xm, xe, xn)


def solution(mesh):
    in_specs = (
        P(("group", "ep"), None),
        P(),
        P(("group", "ep"), None),
        P(("group", "ep"), None),
        P("ep", None, None),
        P("ep", None, None),
        P("ep", None, None),
    )
    out_specs = P(("group", "ep"), None)

    def body(hidden, norm_gain, routes, route_weight, w_gate, w_up, w_down):
        count, tok, picks = mesh.shape["ep"], hidden.shape[0], routes.shape[1]
        dense = count == 16 and w_gate.shape[0] == 1 and 2 * picks >= count
        plan = gather_rows if dense else send_slots
        return plan(hidden, norm_gain, routes, route_weight, w_gate, w_up, w_down)

    return jax.shard_map(body, mesh=mesh, in_specs=in_specs, out_specs=out_specs, check_vma=False)
```

```python
import functools

import jax
import jax.numpy as jnp
from jax import lax
from jax.experimental import pallas as pl
from jax.experimental.pallas import tpu as pltpu
from jax.sharding import PartitionSpec as P


SMALL = pl.CostEstimate(flops=1, bytes_accessed=1, transcendentals=0)


def normalise(hidden, norm_gain):
    xf = hidden.astype(jnp.float32)
    return (xf * lax.rsqrt(jnp.mean(xf * xf, axis=-1, keepdims=True) + 1e-06) * norm_gain).astype(
        jnp.bfloat16
    )


def send_slots(hidden, norm_gain, routes, route_weight, w_gate, w_up, w_down):
    count = lax.axis_size("ep")
    tok = hidden.shape[0]
    width = hidden.shape[1]
    picks = routes.shape[1]
    experts = count * w_gate.shape[0]
    slots = tok * picks * 5 // (4 * experts)
    normed = normalise(hidden, norm_gain)
    share = route_weight / jnp.sum(route_weight, axis=1, keepdims=True)
    flat = routes.reshape(-1)
    onehot = (flat[:, None] == jnp.arange(experts, dtype=jnp.int32)[None, :]).astype(jnp.int32)
    ranked = jnp.cumsum(onehot, axis=0) - onehot
    slot = jnp.sum(ranked * onehot, axis=1)
    token_of = jnp.arange(tok * picks, dtype=jnp.int32) // picks
    outgoing = jnp.zeros((experts, slots, width), jnp.bfloat16).at[flat, slot].set(normed[token_of])
    arrived = lax.all_to_all(outgoing, "ep", split_axis=0, concat_axis=0, tiled=True)
    rows = arrived.reshape(-1, width)
    gate = jnp.dot(rows, w_gate[0], preferred_element_type=jnp.float32)
    upper = jnp.dot(rows, w_up[0], preferred_element_type=jnp.float32)
    units = (jax.nn.silu(gate) * upper).astype(jnp.bfloat16)
    result = jnp.dot(units, w_down[0], preferred_element_type=jnp.float32).astype(jnp.bfloat16)
    coming_back = lax.all_to_all(
        result.reshape(arrived.shape), "ep", split_axis=0, concat_axis=0, tiled=True
    )
    picked = coming_back[flat, slot]
    picked = picked.reshape(tok, picks, width).astype(jnp.float32)
    mixed = jnp.einsum("tk,tkd->td", share, picked)
    return mixed.astype(jnp.bfloat16)


def prepare_kernel(*refs):
    out, sems = refs[4], refs[9]
    hidden, gain, routes, scores = refs[5:9]
    copies = [pltpu.make_async_copy(refs[n], refs[5 + n], sems.at[n]) for n in range(4)]
    for copy in copies:
        copy.start()
    for copy in copies:
        copy.wait()
    f32, bf16 = jnp.float32, jnp.bfloat16
    tok, width = hidden.shape
    x = hidden[...].astype(f32)
    mean = jnp.mean(x * x, axis=-1, keepdims=True)
    out[:, :width] = (x * lax.rsqrt(mean + 1e-06) * gain[...]).astype(bf16)
    score = scores[...].T
    share = score / jnp.sum(score, axis=1, keepdims=True)
    names = routes[...].T
    pad = out.shape[1] - width
    lane = lax.broadcasted_iota(jnp.int32, (tok, pad), 1)
    expert = lane % (pad // 2)
    dense = jnp.zeros((tok, pad), f32)
    for k in range(names.shape[1]):
        dense += jnp.where(expert == names[:, k : k + 1], share[:, k : k + 1], 0.0)
    high = dense.astype(bf16).astype(f32)
    out[:, width:] = jnp.where(lane < pad // 2, high, dense - high).astype(bf16)


def prepare(hidden, norm_gain, routes, route_weight):
    tok, width = hidden.shape
    arrays = (hidden, norm_gain.reshape(1, width), routes.T, route_weight.T)
    return pl.pallas_call(
        prepare_kernel,
        in_specs=[pl.BlockSpec(memory_space=pltpu.HBM)] * 4,
        out_specs=pl.BlockSpec(memory_space=pltpu.VMEM),
        out_shape=jax.ShapeDtypeStruct((tok, width + 128), jnp.bfloat16),
        scratch_shapes=[pltpu.VMEM(array.shape, array.dtype) for array in arrays]
        + [pltpu.SemaphoreType.DMA((4,))],
        compiler_params=pltpu.CompilerParams(vmem_limit_bytes=62 * 2**20),
    )(*arrays)


def hold_kernel(count, *refs):
    token, sems = refs[-2:]
    copies = [pltpu.make_async_copy(refs[n], refs[count + n], sems.at[n]) for n in range(count)]
    for copy in copies:
        copy.start()
    token[...] = jnp.zeros(token.shape, token.dtype)
    for copy in copies:
        copy.wait()


def hold(*arrays):
    count = len(arrays)
    *held, token = pl.pallas_call(
        functools.partial(hold_kernel, count),
        in_specs=[pl.BlockSpec(memory_space=pl.ANY)] * count,
        out_specs=[pl.BlockSpec(memory_space=pltpu.VMEM)] * (count + 1),
        out_shape=[pltpu.VMEM(array.shape, array.dtype) for array in arrays]
        + [jax.ShapeDtypeStruct((8, 128), jnp.float32)],
        scratch_shapes=[pltpu.SemaphoreType.DMA((count,))],
        compiler_params=pltpu.CompilerParams(vmem_limit_bytes=2 * 2**20),
        cost_estimate=SMALL,
    )(*[pltpu.with_memory_space_constraint(array, pltpu.HBM) for array in arrays])
    return held, token


def again_kernel(array, after, out, sem):
    del after
    copy = pltpu.make_async_copy(array, out, sem)
    copy.start()
    copy.wait()


def again(array, after):
    anywhere = pl.BlockSpec(memory_space=pl.ANY)
    return pl.pallas_call(
        again_kernel,
        in_specs=[anywhere] * 2,
        out_specs=anywhere,
        out_shape=jax.ShapeDtypeStruct(array.shape, array.dtype),
        scratch_shapes=[pltpu.SemaphoreType.DMA],
        compiler_params=pltpu.CompilerParams(vmem_limit_bytes=2**20),
        cost_estimate=SMALL,
    )(pltpu.with_memory_space_constraint(array, pltpu.HBM), after)


def gate_kernel(*refs):
    del refs


def gate(through, after):
    count = len(through)
    anywhere = pl.BlockSpec(memory_space=pl.ANY)
    return pl.pallas_call(
        gate_kernel,
        in_specs=[anywhere] * (count + len(after)),
        out_specs=[anywhere] * count,
        out_shape=[jax.ShapeDtypeStruct(array.shape, array.dtype) for array in through],
        input_output_aliases={n: n for n in range(count)},
        compiler_params=pltpu.CompilerParams(vmem_limit_bytes=2**20),
        cost_estimate=SMALL,
    )(*through, *after)


def experts_kernel(count, tile, *refs):
    me = lax.axis_index("ep")
    blocks, weights, outs = refs[:count], refs[count : count + 6], refs[count + 6 : 2 * count + 6]
    rows, total, sems = refs[2 * count + 6 :]
    width = outs[0].shape[1]
    ff = weights[0].shape[2]
    f32, bf16 = jnp.float32, jnp.bfloat16

    copies, at = [], 0
    for n, block in enumerate(blocks):
        size = block.shape[0]
        copies.append(pltpu.make_async_copy(block, rows.at[pl.ds(at, size)], sems.at[n]))
        at += size
    for copy in copies:
        copy.start()
    for copy in copies:
        copy.wait()

    shares = rows[:, width:].astype(f32)
    half = shares.shape[1] // 2
    lane = lax.broadcasted_iota(jnp.int32, shares.shape, 1) % half
    x = rows[:, :width]
    steps = ff // tile
    for j in range(2):
        wg, wu, wd = weights[3 * j : 3 * j + 3]
        share = jnp.sum(jnp.where(lane == (me ^ j), shares, 0.0), axis=1, keepdims=True)
        for t in range(steps):
            some = pl.ds(t * tile, tile)
            gate = jnp.dot(x, wg[0, :, some], preferred_element_type=f32)
            upper = jnp.dot(x, wu[0, :, some], preferred_element_type=f32)
            units = (gate / (1.0 + jnp.exp(-gate)) * upper * share).astype(bf16)
            part = jnp.dot(units, wd[0, some, :], preferred_element_type=f32)
            if j == 0 and t == 0:
                total[...] = part
            elif j == 0 or t < steps - 1:
                total[...] += part
            else:
                done = (total[...] + part).astype(bf16)
                at = 0
                for out in outs:
                    out[...] = done[at : at + out.shape[0]]
                    at += out.shape[0]


def run_experts(blocks, weights):
    count = len(blocks)
    sizes = [block.shape[0] for block in blocks]
    wide = blocks[0].shape[1]
    _, width, ff = weights[0].shape
    whole = sum(sizes)
    vmem, anywhere = pl.BlockSpec(memory_space=pltpu.VMEM), pl.BlockSpec(memory_space=pl.ANY)
    return pl.pallas_call(
        functools.partial(experts_kernel, count, ff // 3),
        in_specs=[anywhere] * count + [vmem] * 6,
        out_specs=[vmem] * count,
        out_shape=[jax.ShapeDtypeStruct((size, width), jnp.bfloat16) for size in sizes],
        scratch_shapes=[
            pltpu.VMEM((whole, wide), jnp.bfloat16),
            pltpu.VMEM((whole, width), jnp.float32),
            pltpu.SemaphoreType.DMA((count,)),
        ],
        compiler_params=pltpu.CompilerParams(vmem_limit_bytes=20 * 2**20),
        cost_estimate=SMALL,
    )(*blocks, *weights)


def choose_kernel(inner, outer, out, sem):
    line = lax.axis_index("ep") // 4
    is_inner = (line == 1) | (line == 2)

    def take(array):
        copy = pltpu.make_async_copy(array, out, sem)
        copy.start()
        copy.wait()

    pl.when(is_inner)(functools.partial(take, inner))
    pl.when(~is_inner)(functools.partial(take, outer))


def choose(inner, outer):
    anywhere = pl.BlockSpec(memory_space=pl.ANY)
    return pl.pallas_call(
        choose_kernel,
        in_specs=[anywhere] * 2,
        out_specs=anywhere,
        out_shape=jax.ShapeDtypeStruct(inner.shape, inner.dtype),
        scratch_shapes=[pltpu.SemaphoreType.DMA],
        compiler_params=pltpu.CompilerParams(vmem_limit_bytes=2**20),
        cost_estimate=SMALL,
    )(inner, outer)


def gather_rows(hidden, norm_gain, routes, route_weight, w_gate, w_up, w_down):
    count = lax.axis_size("ep")
    f32, bf16 = jnp.float32, jnp.bfloat16
    tie = lambda *arrays: lax.optimization_barrier(arrays)

    def line(x, to):
        moves = [(i, to[i // 4] * 4 + i % 4) for i in range(count) if to[i // 4] is not None]
        return lax.ppermute(x, "ep", moves)

    def cross(x):
        return lax.ppermute(x, "ep", [(i, i ^ 2) for i in range(count)])

    def other_core(x):
        return lax.ppermute(x, "ep", [(i, i ^ 1) for i in range(count)])

    def add(*parts):
        return sum(p.astype(f32) for p in parts).astype(bf16)

    far, back = [2, 0, 3, 1], [1, 3, 0, 2]
    pairs, middle = [1, 0, 3, 2], [None, 2, 1, None]
    outward, inward = [None, 0, 3, None], [1, None, None, 2]
    far_ends = [None, 3, 0, None]

    far_gate, far_up = other_core(w_gate), other_core(w_up)
    own = prepare(hidden, norm_gain, routes, route_weight)

    a, y0 = line(own, far), cross(own)
    weights, token = hold(w_gate, w_up, w_down)
    a, y0, far_gate, far_up = gate([a, y0, far_gate, far_up], [token])

    b, n, ya = line(choose(a, own), pairs), line(own, middle), cross(a)
    far_down = other_core(w_down)
    held, token = hold(far_gate, far_up, far_down)
    weights += held
    b, n, ya = gate([b, n, ya], [token])

    c, yb = line(n, outward), cross(b)
    m0, o0 = run_experts([own, y0], weights)
    ma, oa = run_experts([a, ya], weights)
    c, yb = gate([c, yb], [o0, oa])

    c = choose(n, c)
    yc = cross(c)
    mb, ob = run_experts([b, yb], weights)
    yc, ob, oa = gate([yc, ob, oa], [])

    place = lax.axis_index("ep") // 4
    is_inner = (place == 1) | (place == 2)

    yob, xo = cross(ob), line(oa, back)
    mc, oc = run_experts([c, yc], weights)
    yob, oc = gate([yob, oc], [])

    yoc, p = cross(oc), line(add(mb, yob), pairs)
    o0 = add(o0, xo)
    yoc, p, o0 = gate([yoc, p, o0], [])

    yo0 = cross(o0)
    rc = add(mc, yoc)
    q, xm = line(rc, inward), line(add(ma, p), far_ends)
    m0 = add(m0, jnp.where(is_inner, jnp.zeros_like(p), p))
    yo0, q, xm, ma, m0 = gate([yo0, q, xm, ma, m0], [])

    xe, xn = line(ma, inward), line(add(rc, q), middle)
    return add(m0, yo0, xm, xe, xn)


def solution(mesh):
    in_specs = (
        P(("group", "ep"), None),
        P(),
        P(("group", "ep"), None),
        P(("group", "ep"), None),
        P("ep", None, None),
        P("ep", None, None),
        P("ep", None, None),
    )
    out_specs = P(("group", "ep"), None)

    def body(hidden, norm_gain, routes, route_weight, w_gate, w_up, w_down):
        count, tok, picks = mesh.shape["ep"], hidden.shape[0], routes.shape[1]
        dense = count == 16 and w_gate.shape[0] == 1 and 2 * picks >= count
        plan = gather_rows if dense else send_slots
        return plan(hidden, norm_gain, routes, route_weight, w_gate, w_up, w_down)

    return jax.shard_map(body, mesh=mesh, in_specs=in_specs, out_specs=out_specs, check_vma=False)
```
